32 devices in a mesh: groups: 2 (over y), row: 8 (over z, x), col: 2 (over core).
Axes of the slice: x: 2, y: 2, z: 4, core: 2. Of those that a mesh axis runs over, the one named last changes fastest.
Arguments:
- tokens: bfloat16 [512, 4096], P('groups', 'col'), parts along dimension 0, may hold values from -6 to 6
- teacher: bfloat16 [512, 4096], P(('groups', 'row'), 'col'), parts along dimension 0, may hold values from -3 to 3
- gate_weight: bfloat16 [4096, 16384], P('col', 'row'), may hold values from -0.09375 to 0.09375
- up_weight: bfloat16 [4096, 16384], P('col', 'row'), may hold values from -0.09375 to 0.09375
- down_weight: bfloat16 [16384, 4096], P('row', 'col'), may hold values from -0.046875 to 0.046875
Outputs:
- student_out: bfloat16 [512, 4096], P(('groups', 'row'), 'col'), parts along dimension 0
- d_tokens: bfloat16 [512, 4096], P(('groups', 'row'), 'col'), parts along dimension 0
- grad_gate: bfloat16 [8192, 16384], P(('groups', 'col'), 'row'), parts along dimension 0
- grad_up: bfloat16 [8192, 16384], P(('groups', 'col'), 'row'), parts along dimension 0
- grad_down: bfloat16 [32768, 4096], P(('groups', 'row'), 'col'), parts along dimension 0
The draws below stay inside these ranges and needn't reach their ends.
There are 2 independent parts, one for each index of `groups`. The reference program is written for one: setup_inputs(seed, part) draws one part's arguments, and reference() takes and returns one part's arrays. A program takes and returns all parts, laid end to end along the dimension named above; an argument that names none is the same for every part. Nothing has to cross between parts.
All inputs are finite; a program needn't handle non-finite values.
Results may differ from the reference program's by a relative error of at most 0.0063.
Values may be sent and summed in bfloat16 or wider, within the bound.
A program may use at most 192 MiB of HBM per device.

```python
import jax
import jax.numpy as jnp

D = 4096
FF = 16384
TOKENS = 256


def block_scale(key, dims, shards, least, high):
    def one(position, parts):
        heights = jax.random.uniform(jax.random.fold_in(jax.random.fold_in(key, 6), position), (parts,), jnp.float32, least / len(shards), high / len(shards))
        return jnp.repeat(jnp.exp(heights), dims[position] // parts).reshape((-1,) + (1,) * (len(dims) - position - 1))

    gain = one(*shards[0])
    for cut in shards[1:]:
        gain = gain * one(*cut)
    return gain


def scatter_about(rng, extent, width, most, split=(), held_as=jnp.bfloat16):
    entries = jax.random.normal(rng, extent, jnp.float32) * width
    if len(split) > 0:
        entries = block_scale(rng, extent, split, -0.22, 0.18) * entries
    return jnp.clip(entries, min=-most, max=most).astype(held_as)


def setup_inputs(seed: int = 0, part: int = 0) -> dict:
    keys = jax.random.split(jax.random.key(seed), 6)
    part_splits = jax.random.split(jax.random.fold_in(keys[5], part), 6)
    return {
        "tokens": scatter_about(part_splits[0], (TOKENS, D), 1.0, 6.0, ((1, 2),)),
        "teacher": scatter_about(part_splits[1], (TOKENS, D), 0.5, 3.0, ((0, 8), (1, 2))),
        "gate_weight": scatter_about(keys[2], (D, FF), D ** -0.5, 0.09375, ((0, 2), (1, 8))),
        "up_weight": scatter_about(keys[3], (D, FF), D ** -0.5, 0.09375, ((0, 2), (1, 8))),
        "down_weight": scatter_about(keys[4], (FF, D), FF ** -0.5, 0.046875, ((0, 8), (1, 2))),
    }


def reference(tokens, teacher, gate_weight, up_weight, down_weight):
    gate_proj = jnp.dot(tokens, gate_weight, preferred_element_type=jnp.float32)
    up_proj = jnp.dot(tokens, up_weight, preferred_element_type=jnp.float32)
    sigmoid_gate = jax.nn.sigmoid(gate_proj)
    activated = gate_proj * sigmoid_gate
    hidden = (activated * up_proj).astype(jnp.bfloat16)
    student = jnp.dot(hidden, down_weight, preferred_element_type=jnp.float32)
    student_out = student.astype(jnp.bfloat16)
    d_student = (student - teacher.astype(jnp.float32)).astype(jnp.bfloat16)
    d_hidden = jnp.dot(d_student, down_weight.T, preferred_element_type=jnp.float32)
    grad_down = jnp.dot(hidden.T, d_student, preferred_element_type=jnp.float32).astype(jnp.bfloat16)
    d_gate = (d_hidden * up_proj * sigmoid_gate * (1.0 + gate_proj * (1.0 - sigmoid_gate))).astype(jnp.bfloat16)
    d_up = (d_hidden * activated).astype(jnp.bfloat16)
    grad_gate = jnp.dot(tokens.T, d_gate, preferred_element_type=jnp.float32).astype(jnp.bfloat16)
    grad_up = jnp.dot(tokens.T, d_up, preferred_element_type=jnp.float32).astype(jnp.bfloat16)
    d_tokens = (jnp.dot(d_gate, gate_weight.T, preferred_element_type=jnp.float32)
                + jnp.dot(d_up, up_weight.T, preferred_element_type=jnp.float32)).astype(jnp.bfloat16)
    return student_out, d_tokens, grad_gate, grad_up, grad_down
```

```python
import jax
import jax.numpy as jnp
from jax import lax
from jax.experimental import pallas as pl
from jax.experimental.pallas import tpu as pltpu
from jax.sharding import PartitionSpec as P

F32 = jnp.float32
BF = jnp.bfloat16
MESH = pl.DeviceIdType.MESH
FCH = 256
NC = 4
ORDER = ("A0", "A1", "A2", "B0", "A3", "B1", "C0", "B2", "C1", "B3", "C2", "C3")


def nt(a, b):
    return lax.dot_general(a, b, (((1,), (1,)), ((), ())), preferred_element_type=F32)


def tn(a, b):
    return lax.dot_general(a, b, (((0,), (0,)), ((), ())), preferred_element_type=F32)


def kernel(
    tokens_h, teacher_ref, wg_h, wu_h, wd_h,
    out_ref, dtok_ref, hid_h, ds_h, dg_h, du_h,
    tok, wg, wu, wd, gp, up, gus, gur, hid,
    pf, pb, xr, sf, zs, za, zb, dsf, dh, dhs, dhr, dg, du,
    pf2, pb2, xr2, zs2, za2, zb2,
    ld_tok, ld_g, ld_u, ld_d, st,
    gu_ss, gu_rs, dh_ss, dh_rs,
    x_ss, x_rs, za_ss, za_rs, zb_ss, zb_rs, ze_ss, ze_rs,
    agz_ss, agz_rs, agm_ss, agx_ss, agx_rs,
):
    r = lax.axis_index("row")
    core = lax.axis_index("col")
    z = r // 2
    x = r % 2
    hi = z // 2
    is_end = jnp.logical_or(z == 0, z == 3)
    is_mid = jnp.logical_not(is_end)
    nz = z + 1 - 2 * (z % 2)
    xid = {"row": z * 2 + 1 - x}
    nid = {"row": nz * 2 + x}
    mid = {"row": (3 - z) * 2 + x}
    cid = {"col": 1 - core}
    end_b = 3 * hi
    far = 2 - 2 * hi
    near = 2 * hi
    three = 1 - hi
    far_m = 2 - hi
    far_e = 3 - 3 * hi
    nff = wg.shape[1]
    nd = wd.shape[1]
    nj = nff // FCH
    cw = nd // NC
    dcw = wg.shape[0] // NC

    def fcols(j):
        return pl.ds(pl.multiple_of(j * FCH, FCH), FCH)

    def cols(c):
        return pl.ds(c * cw, cw)

    pltpu.make_async_copy(tokens_h, tok, ld_tok).start()
    for j in range(nj):
        s = pl.ds(j * FCH, FCH)
        pltpu.make_async_copy(wg_h.at[:, s], wg.at[:, s], ld_g.at[j]).start()
        pltpu.make_async_copy(wu_h.at[:, s], wu.at[:, s], ld_u.at[j]).start()
    for c in range(NC):
        pltpu.make_async_copy(wd_h.at[:, cols(c)], wd.at[:, cols(c)], ld_d.at[c]).start()

    barrier = pltpu.get_barrier_semaphore()
    pl.semaphore_signal(barrier, inc=1, device_id=cid, device_id_type=MESH)
    pl.semaphore_signal(barrier, inc=1, device_id=xid, device_id_type=MESH)
    pl.semaphore_signal(barrier, inc=1, device_id=nid, device_id_type=MESH)

    @pl.when(is_mid)
    def _():
        pl.semaphore_signal(barrier, inc=1, device_id=mid, device_id_type=MESH)
        pl.semaphore_wait(barrier, 4)

    @pl.when(is_end)
    def _():
        pl.semaphore_wait(barrier, 3)

    def rc(src, dst, ss, rs, dev):
        return pltpu.make_async_remote_copy(
            src_ref=src, dst_ref=dst, send_sem=ss, recv_sem=rs, device_id=dev, device_id_type=MESH
        )

    def gu_copy(j):
        return rc(gus.at[j], gur.at[j], gu_ss.at[j], gu_rs.at[j], cid)

    pltpu.make_async_copy(tokens_h, tok, ld_tok).wait()

    def first(j, carry):
        s = fcols(j)
        pltpu.make_async_copy(wg_h.at[:, s], wg.at[:, s], ld_g.at[j]).wait()
        pg = jnp.dot(tok[...], wg[:, s], preferred_element_type=F32)
        gp[:, s] = pg
        gus[j, 0] = pg.astype(BF)
        pltpu.make_async_copy(wu_h.at[:, s], wu.at[:, s], ld_u.at[j]).wait()
        pu = jnp.dot(tok[...], wu[:, s], preferred_element_type=F32)
        up[:, s] = pu
        gus[j, 1] = pu.astype(BF)
        gu_copy(j).start()
        return carry

    lax.fori_loop(0, nj, first, 0)

    def second(j, carry):
        s = fcols(j)
        gu_copy(j).wait_recv()
        g = gp[:, s] + gur[j, 0].astype(F32)
        u = up[:, s] + gur[j, 1].astype(F32)
        gp[:, s] = g
        up[:, s] = u
        hid[:, s] = (g * jax.nn.sigmoid(g) * u).astype(BF)
        return carry

    lax.fori_loop(0, nj, second, 0)
    pltpu.make_async_copy(hid, hid_h, st.at[0]).start()

    def x_copy(k, c):
        b, t = (pb, xr) if k == 0 else (pb2, xr2)
        return rc(b.at[:, 1 - x, :, cols(c)], t.at[:, :, cols(c)], x_ss.at[k, c], x_rs.at[k, c], xid)

    def in_copy(k, c):
        b, t = (zs, za) if k == 0 else (zs2, za2)
        return rc(b.at[pl.ds(three, 3), :, cols(c)], t.at[pl.ds(three, 3), :, cols(c)], za_ss.at[k, c], za_rs.at[k, c], nid)

    def mid_copy(k, c, start):
        b, t = (zs, zb) if k == 0 else (zs2, zb2)
        return rc(b.at[pl.ds(start, 2), :, cols(c)], t.at[pl.ds(start, 2), :, cols(c)], zb_ss.at[k, c], zb_rs.at[k, c], mid)

    def out_copy(k, c):
        b, t = (zs, za) if k == 0 else (zs2, za2)
        return rc(b.at[pl.ds(end_b, 1), :, cols(c)], t.at[pl.ds(end_b, 1), :, cols(c)], ze_ss.at[k, c], ze_rs.at[k, c], nid)

    def stage_a(k, c):
        f, t = (pf, xr) if k == 0 else (pf2, xr2)
        b, a = (zs, za) if k == 0 else (zs2, za2)
        q = cols(c)
        x_copy(k, c).wait_recv()
        sf[:, :, q] = f[:, x, :, q] + t[:, :, q].astype(F32)

        @pl.when(is_end)
        def _():
            b[pl.ds(three, 3), :, q] = sf[pl.ds(three, 3), :, q].astype(BF)
            in_copy(k, c).start()

        @pl.when(is_mid)
        def _():
            in_copy(k, c).wait_recv()
            m = pl.ds(far, 2)
            b[m, :, q] = (sf[m, :, q] + a[m, :, q].astype(F32)).astype(BF)
            mid_copy(k, c, far).start()

    def stage_b(k, c, final):
        b, a, m = (zs, za, zb) if k == 0 else (zs2, za2, zb2)
        q = cols(c)

        @pl.when(is_end)
        def _():
            out_copy(k, c).wait_recv()
            final(c, sf[z, :, q] + a[z, :, q].astype(F32))

        @pl.when(is_mid)
        def _():
            mid_copy(k, c, near).wait_recv()
            b[end_b, :, q] = (sf[end_b, :, q] + m[end_b, :, q].astype(F32)).astype(BF)
            out_copy(k, c).start()
            final(c, sf[z, :, q] + a[z, :, q].astype(F32) + m[z, :, q].astype(F32))

    def rs_drain(k):
        for c in range(NC):
            x_copy(k, c).wait_send()

            @pl.when(is_end)
            def _():
                in_copy(k, c).wait_send()

            @pl.when(is_mid)
            def _():
                mid_copy(k, c, far).wait_send()
                out_copy(k, c).wait_send()

    for c in range(NC):
        q = cols(c)
        pltpu.make_async_copy(wd_h.at[:, q], wd.at[:, q], ld_d.at[c]).wait()
        pc = jnp.dot(hid[...], wd[:, q], preferred_element_type=F32).reshape(4, 2, 32, cw)
        pf[:, :, :, q] = pc
        pb[:, :, :, q] = pc.astype(BF)
        x_copy(0, c).start()

    def factors(j, carry):
        s = fcols(j)
        g = gp[:, s]
        u = up[:, s]
        sg = jax.nn.sigmoid(g)
        gp[:, s] = u * sg * (1.0 + g * (1.0 - sg))
        up[:, s] = g * sg
        return carry

    lax.fori_loop(0, nj, factors, 0)

    def agz(c, t):
        b = dsf.at[t * 2 + x, :, cols(c)]
        return rc(b, b, agz_ss.at[c, t], agz_rs.at[c, t], nid)

    def agm(c, t):
        b = dsf.at[t * 2 + x, :, cols(c)]
        return rc(b, b, agm_ss.at[c, t], agz_rs.at[c, t], mid)

    def agx(c, t, src_x):
        b = dsf.at[t * 2 + src_x, :, cols(c)]
        return rc(b, b, agx_ss.at[c, t], agx_rs.at[c, t], xid)

    def student_final(c, v):
        q = cols(c)
        out_ref[:, q] = v.astype(BF)
        dsf[r, :, q] = (v - teacher_ref[:, q].astype(F32)).astype(BF)
        agz(c, z).start()
        pl.when(is_mid)(lambda: agm(c, z).start())
        agx(c, z, x).start()

    def stage_c(c):
        @pl.when(is_end)
        def _():
            agz(c, nz).wait_recv()
            agx(c, nz, x).start()
            agz(c, far_m).wait_recv()
            agx(c, far_m, x).start()
            agz(c, far_e).wait_recv()
            agx(c, far_e, x).start()

        @pl.when(is_mid)
        def _():
            agz(c, nz).wait_recv()
            agm(c, nz).start()
            agx(c, nz, x).start()
            agm(c, far_m).wait_recv()
            agz(c, far_m).start()
            agx(c, far_m, x).start()
            agm(c, far_e).wait_recv()
            agz(c, far_e).start()
            agx(c, far_e, x).start()

    for step in ORDER:
        c = int(step[1])
        if step[0] == "A":
            stage_a(0, c)
        elif step[0] == "B":
            stage_b(0, c, student_final)
        else:
            stage_c(c)
    for c in range(NC):
        for t in range(4):
            agx(c, t, 1 - x).wait_recv()
    ds_copy = pltpu.make_async_copy(dsf, ds_h, st.at[1])
    ds_copy.start()

    def dh_copy(j):
        return rc(dhs.at[j], dhr.at[j], dh_ss.at[j], dh_rs.at[j], cid)

    def third(j, carry):
        p = nt(dsf[...].reshape(256, nd), wd[fcols(j), :])
        dh[j] = p
        dhs[j] = p.astype(BF)
        dh_copy(j).start()
        return carry

    lax.fori_loop(0, nj, third, 0)

    def fourth(j, carry):
        s = fcols(j)
        dh_copy(j).wait_recv()
        d = dh[j] + dhr[j].astype(F32)
        dg[:, s] = (d * gp[:, s]).astype(BF)
        du[:, s] = (d * up[:, s]).astype(BF)
        return carry

    lax.fori_loop(0, nj, fourth, 0)
    pltpu.make_async_copy(dg, dg_h, st.at[2]).start()
    pltpu.make_async_copy(du, du_h, st.at[3]).start()

    for c in range(NC):
        q = cols(c)
        pc = (nt(dg[...], wg[q, :]) + nt(du[...], wu[q, :])).reshape(4, 2, 32, cw)
        pf2[:, :, :, q] = pc
        pb2[:, :, :, q] = pc.astype(BF)
        x_copy(1, c).start()

    def dtok_final(c, v):
        dtok_ref[:, cols(c)] = v.astype(BF)

    for step in ORDER:
        c = int(step[1])
        if step[0] == "A":
            stage_a(1, c)
        elif step[0] == "B":
            stage_b(1, c, dtok_final)

    def drain(j, carry):
        gu_copy(j).wait_send()
        dh_copy(j).wait_send()
        return carry

    lax.fori_loop(0, nj, drain, 0)
    rs_drain(0)
    rs_drain(1)
    for c in range(NC):
        agz(c, z).wait_send()
        for t in range(4):
            agx(c, t, x).wait_send()

        @pl.when(is_mid)
        def _():
            agm(c, z).wait_send()
            agm(c, nz).wait_send()
            agz(c, far_m).wait_send()
            agz(c, far_e).wait_send()

    for i, (a, b) in enumerate(((hid, hid_h), (dsf, ds_h), (dg, dg_h), (du, du_h))):
        pltpu.make_async_copy(a, b, st.at[i]).wait()


def fused(tokens, teacher, gate_weight, up_weight, down_weight):
    m, d = tokens.shape
    ff = gate_weight.shape[1]
    rows = teacher.shape[0]
    nj = ff // FCH
    V = pltpu.VMEM
    D = pltpu.SemaphoreType.DMA
    rs_set = [V((4, rows, d), BF)] * 3
    scratch = [
        V((m, d), BF), V((d, ff), BF), V((d, ff), BF), V((ff, d), BF),
        V((m, ff), F32), V((m, ff), F32),
        V((nj, 2, m, FCH), BF), V((nj, 2, m, FCH), BF), V((m, ff), BF),
        V((4, 2, rows, d), F32), V((4, 2, rows, d), BF), V((4, rows, d), BF), V((4, rows, d), F32),
        *rs_set, V((8, rows, d), BF),
        V((nj, m, FCH), F32), V((nj, m, FCH), BF), V((nj, m, FCH), BF),
        V((m, ff), BF), V((m, ff), BF),
        V((4, 2, rows, d), F32), V((4, 2, rows, d), BF), V((4, rows, d), BF), *rs_set,
        D, D((nj,)), D((nj,)), D((NC,)), D((4,)),
        D((nj,)), D((nj,)), D((nj,)), D((nj,)),
        *([D((2, NC))] * 8),
        *([D((NC, 4))] * 5),
    ]
    hbm = pl.BlockSpec(memory_space=pl.ANY)
    vm = pl.BlockSpec(memory_space=pltpu.VMEM)
    flops = 2 * m * d * ff * 6
    return pl.pallas_call(
        kernel,
        out_shape=(
            jax.ShapeDtypeStruct((rows, d), BF), jax.ShapeDtypeStruct((rows, d), BF),
            jax.ShapeDtypeStruct((m, ff), BF), jax.ShapeDtypeStruct((8, rows, d), BF),
            jax.ShapeDtypeStruct((m, ff), BF), jax.ShapeDtypeStruct((m, ff), BF),
        ),
        in_specs=[hbm, vm, hbm, hbm, hbm],
        out_specs=(vm, vm, hbm, hbm, hbm, hbm),
        scratch_shapes=scratch,
        compiler_params=pltpu.CompilerParams(
            collective_id=0, has_side_effects=True, vmem_limit_bytes=62 * 1024 * 1024
        ),
        cost_estimate=pl.CostEstimate(flops=flops, bytes_accessed=6 * d * ff, transcendentals=m * ff),
        name="chain",
    )(tokens, teacher, gate_weight, up_weight, down_weight)


def local_fused(tokens, teacher, gate_weight, up_weight, down_weight):
    out, dtok, hid, ds, dg, du = fused(tokens, teacher, gate_weight, up_weight, down_weight)
    ds = ds.reshape(tokens.shape)
    grad_down = tn(hid, ds).astype(BF)
    grad_gate = tn(tokens, dg).astype(BF)
    grad_up = tn(tokens, du).astype(BF)
    return out, dtok, grad_gate, grad_up, grad_down


def local(tokens, teacher, gate_weight, up_weight, down_weight):
    local_rows = teacher.shape[0]
    part_gate = jnp.dot(tokens, gate_weight, preferred_element_type=F32)
    part_up = jnp.dot(tokens, up_weight, preferred_element_type=F32)
    gate_proj, up_proj = lax.psum((part_gate, part_up), "col")
    sigmoid_gate = jax.nn.sigmoid(gate_proj)
    activated = gate_proj * sigmoid_gate
    hidden = (activated * up_proj).astype(BF)
    partial_out = jnp.dot(hidden, down_weight, preferred_element_type=F32)
    student = lax.psum(partial_out, "row")
    own_start = lax.axis_index("row") * local_rows
    own_rows = lax.dynamic_slice_in_dim(student, own_start, local_rows, 0)
    student_out = own_rows.astype(BF)
    teacher_all = lax.all_gather(teacher, "row", axis=0, tiled=True)
    d_student = (student - teacher_all.astype(F32)).astype(BF)
    d_hidden = lax.psum(nt(d_student, down_weight), "col")
    grad_down = tn(hidden, d_student).astype(BF)
    d_gate = (d_hidden * up_proj * sigmoid_gate * (1.0 + gate_proj * (1.0 - sigmoid_gate))).astype(BF)
    d_up = (d_hidden * activated).astype(BF)
    grad_gate = tn(tokens, d_gate).astype(BF)
    grad_up = tn(tokens, d_up).astype(BF)
    total = nt(d_gate, gate_weight) + nt(d_up, up_weight)
    d_tokens = lax.psum_scatter(total, "row", scatter_dimension=0, tiled=True).astype(BF)
    return (student_out, d_tokens, grad_gate, grad_up, grad_down)


def solution(mesh):
    placed = (
        P("groups", "col"),
        P(("groups", "row"), "col"),
        P("col", "row"),
        P("col", "row"),
        P("row", "col"),
    )
    small = mesh.shape["row"] == 8 and mesh.shape["col"] == 2
    return jax.shard_map(
        local_fused if small else local,
        mesh=mesh,
        in_specs=placed,
        out_specs=(
            P(("groups", "row"), "col"),
            P(("groups", "row"), "col"),
            P(("groups", "col"), "row"),
            P(("groups", "col"), "row"),
            P(("groups", "row"), "col"),
        ),
        check_vma=False,
    )
```

```python
import jax
import jax.numpy as jnp
from jax import lax
from jax.experimental import pallas as pl
from jax.experimental.pallas import tpu as pltpu
from jax.sharding import PartitionSpec as P

F32 = jnp.float32
BF = jnp.bfloat16
MESH = pl.DeviceIdType.MESH
FCH = 512
NC = 4
LAG_B = 1
LAG_C = 2


def nt(a, b):
    return lax.dot_general(a, b, (((1,), (1,)), ((), ())), preferred_element_type=F32)


def tn(a, b):
    return lax.dot_general(a, b, (((0,), (0,)), ((), ())), preferred_element_type=F32)


def kernel(
    tokens_h, teacher_ref, wg_h, wu_h, wd_h,
    out_ref, dtok_ref, hid_h, ds_h, dg_h, du_h,
    tok, wg, wu, wd, gp, up, gus, gur, hid,
    pf, pb, xr, sf, zs, zr, dsf, dh, dhs, dhr, dg, du,
    pf2, pb2, xr2, zs2, zr2,
    ld_tok, ld_g, ld_u, ld_d, st,
    gu_ss, gu_rs, dh_ss, dh_rs,
    x_ss, x_rs, z_ss, z_rs, agz_ss, agz_rs, agx_ss, agx_rs,
):
    r = lax.axis_index("row")
    core = lax.axis_index("col")
    z = r // 2
    x = r % 2
    xid = {"row": z * 2 + 1 - x}
    cid = {"col": 1 - core}
    others = [(z + i) % 4 for i in (1, 2, 3)]
    nff = wg.shape[1]
    nd = wd.shape[1]
    nj = nff // FCH
    cw = nd // NC
    dcw = wg.shape[0] // NC

    def fcols(j):
        return pl.ds(pl.multiple_of(j * FCH, FCH), FCH)

    def cols(c):
        return pl.ds(c * cw, cw)

    pltpu.make_async_copy(tokens_h, tok, ld_tok).start()
    for j in range(nj):
        s = pl.ds(j * FCH, FCH)
        pltpu.make_async_copy(wg_h.at[:, s], wg.at[:, s], ld_g.at[j]).start()
        pltpu.make_async_copy(wu_h.at[:, s], wu.at[:, s], ld_u.at[j]).start()
    for c in range(NC):
        pltpu.make_async_copy(wd_h.at[:, cols(c)], wd.at[:, cols(c)], ld_d.at[c]).start()

    barrier = pltpu.get_barrier_semaphore()
    pl.semaphore_signal(barrier, inc=1, device_id=cid, device_id_type=MESH)
    pl.semaphore_signal(barrier, inc=1, device_id=xid, device_id_type=MESH)
    for t in others:
        pl.semaphore_signal(barrier, inc=1, device_id={"row": t * 2 + x}, device_id_type=MESH)
    pl.semaphore_wait(barrier, 5)

    def rc(src, dst, ss, rs, dev):
        return pltpu.make_async_remote_copy(
            src_ref=src, dst_ref=dst, send_sem=ss, recv_sem=rs, device_id=dev, device_id_type=MESH
        )

    def gu_copy(j):
        return rc(gus.at[j], gur.at[j], gu_ss.at[j], gu_rs.at[j], cid)

    pltpu.make_async_copy(tokens_h, tok, ld_tok).wait()

    def first(j, carry):
        s = fcols(j)
        pltpu.make_async_copy(wg_h.at[:, s], wg.at[:, s], ld_g.at[j]).wait()
        pg = jnp.dot(tok[...], wg[:, s], preferred_element_type=F32)
        gp[:, s] = pg
        gus[j, 0] = pg.astype(BF)
        pltpu.make_async_copy(wu_h.at[:, s], wu.at[:, s], ld_u.at[j]).wait()
        pu = jnp.dot(tok[...], wu[:, s], preferred_element_type=F32)
        up[:, s] = pu
        gus[j, 1] = pu.astype(BF)
        gu_copy(j).start()
        return carry

    lax.fori_loop(0, nj, first, 0)

    def second(j, carry):
        s = fcols(j)
        gu_copy(j).wait_recv()
        g = gp[:, s] + gur[j, 0].astype(F32)
        u = up[:, s] + gur[j, 1].astype(F32)
        gp[:, s] = g
        up[:, s] = u
        hid[:, s] = (g * jax.nn.sigmoid(g) * u).astype(BF)
        return carry

    lax.fori_loop(0, nj, second, 0)
    pltpu.make_async_copy(hid, hid_h, st.at[0]).start()

    def x_copy(k, c):
        b, t = (pb, xr) if k == 0 else (pb2, xr2)
        return rc(b.at[:, 1 - x, :, cols(c)], t.at[:, :, cols(c)], x_ss.at[k, c], x_rs.at[k, c], xid)

    def z_send(k, c, t):
        b, s = (zs, zr) if k == 0 else (zs2, zr2)
        return rc(b.at[t, :, cols(c)], s.at[z, :, cols(c)], z_ss.at[k, c, t], z_rs.at[k, c, z], {"row": t * 2 + x})

    def z_recv(k, c, t):
        b, s = (zs, zr) if k == 0 else (zs2, zr2)
        return rc(b.at[t, :, cols(c)], s.at[t, :, cols(c)], z_ss.at[k, c, t], z_rs.at[k, c, t], {"row": t * 2 + x})

    def stage_a(k, c):
        f, t, b = (pf, xr, zs) if k == 0 else (pf2, xr2, zs2)
        q = cols(c)
        x_copy(k, c).wait_recv()
        v = f[:, x, :, q] + t[:, :, q].astype(F32)
        sf[:, :, q] = v
        b[:, :, q] = v.astype(BF)
        for o in others:
            z_send(k, c, o).start()

    def stage_b(k, c, final):
        s = zr if k == 0 else zr2
        q = cols(c)
        v = sf[z, :, q]
        for o in others:
            z_recv(k, c, o).wait_recv()
            v = v + s[o, :, q].astype(F32)
        final(c, v)

    def rs_drain(k):
        for c in range(NC):
            x_copy(k, c).wait_send()
            for o in others:
                z_send(k, c, o).wait_send()

    for c in range(NC):
        q = cols(c)
        pltpu.make_async_copy(wd_h.at[:, q], wd.at[:, q], ld_d.at[c]).wait()
        pc = jnp.dot(hid[...], wd[:, q], preferred_element_type=F32).reshape(4, 2, 32, cw)
        pf[:, :, :, q] = pc
        pb[:, :, :, q] = pc.astype(BF)
        x_copy(0, c).start()

    def factors(j, carry):
        s = fcols(j)
        g = gp[:, s]
        u = up[:, s]
        sg = jax.nn.sigmoid(g)
        gp[:, s] = u * sg * (1.0 + g * (1.0 - sg))
        up[:, s] = g * sg
        return carry

    lax.fori_loop(0, nj, factors, 0)

    def agz_send(c, t):
        b = dsf.at[r, :, cols(c)]
        return rc(b, b, agz_ss.at[c, t], agz_rs.at[c, z], {"row": t * 2 + x})

    def agz_recv(c, t):
        b = dsf.at[t * 2 + x, :, cols(c)]
        return rc(b, b, agz_ss.at[c, t], agz_rs.at[c, t], {"row": t * 2 + x})

    def agx(c, t, src_x):
        b = dsf.at[t * 2 + src_x, :, cols(c)]
        return rc(b, b, agx_ss.at[c, t], agx_rs.at[c, t], xid)

    def student_final(c, v):
        q = cols(c)
        out_ref[:, q] = v.astype(BF)
        dsf[r, :, q] = (v - teacher_ref[:, q].astype(F32)).astype(BF)
        agx(c, z, x).start()
        for o in others:
            agz_send(c, o).start()

    def stage_c(c):
        for o in others:
            agz_recv(c, o).wait_recv()
            agx(c, o, x).start()

    for i in range(NC + LAG_C):
        if i < NC:
            stage_a(0, i)
        if 0 <= i - LAG_B < NC:
            stage_b(0, i - LAG_B, student_final)
        if 0 <= i - LAG_C < NC:
            stage_c(i - LAG_C)
    for c in range(NC):
        for t in range(4):
            agx(c, t, 1 - x).wait_recv()
    ds_copy = pltpu.make_async_copy(dsf, ds_h, st.at[1])
    ds_copy.start()

    def dh_copy(j):
        return rc(dhs.at[j], dhr.at[j], dh_ss.at[j], dh_rs.at[j], cid)

    def third(j, carry):
        p = nt(dsf[...].reshape(256, nd), wd[fcols(j), :])
        dh[j] = p
        dhs[j] = p.astype(BF)
        dh_copy(j).start()
        return carry

    lax.fori_loop(0, nj, third, 0)

    def fourth(j, carry):
        s = fcols(j)
        dh_copy(j).wait_recv()
        d = dh[j] + dhr[j].astype(F32)
        dg[:, s] = (d * gp[:, s]).astype(BF)
        du[:, s] = (d * up[:, s]).astype(BF)
        return carry

    lax.fori_loop(0, nj, fourth, 0)
    pltpu.make_async_copy(dg, dg_h, st.at[2]).start()
    pltpu.make_async_copy(du, du_h, st.at[3]).start()

    for c in range(NC):
        q = cols(c)
        pc = (nt(dg[...], wg[q, :]) + nt(du[...], wu[q, :])).reshape(4, 2, 32, cw)
        pf2[:, :, :, q] = pc
        pb2[:, :, :, q] = pc.astype(BF)
        x_copy(1, c).start()

    def dtok_final(c, v):
        dtok_ref[:, cols(c)] = v.astype(BF)

    for i in range(NC + LAG_B):
        if i < NC:
            stage_a(1, i)
        if i >= LAG_B:
            stage_b(1, i - LAG_B, dtok_final)

    def drain(j, carry):
        gu_copy(j).wait_send()
        dh_copy(j).wait_send()
        return carry

    lax.fori_loop(0, nj, drain, 0)
    rs_drain(0)
    rs_drain(1)
    for c in range(NC):
        for o in others:
            agz_send(c, o).wait_send()
        for t in range(4):
            agx(c, t, x).wait_send()

    for i, (a, b) in enumerate(((hid, hid_h), (dsf, ds_h), (dg, dg_h), (du, du_h))):
        pltpu.make_async_copy(a, b, st.at[i]).wait()


def fused(tokens, teacher, gate_weight, up_weight, down_weight):
    m, d = tokens.shape
    ff = gate_weight.shape[1]
    rows = teacher.shape[0]
    nj = ff // FCH
    V = pltpu.VMEM
    D = pltpu.SemaphoreType.DMA
    rs_set = [V((4, rows, d), BF)] * 2
    scratch = [
        V((m, d), BF), V((d, ff), BF), V((d, ff), BF), V((ff, d), BF),
        V((m, ff), F32), V((m, ff), F32),
        V((nj, 2, m, FCH), BF), V((nj, 2, m, FCH), BF), V((m, ff), BF),
        V((4, 2, rows, d), F32), V((4, 2, rows, d), BF), V((4, rows, d), BF), V((4, rows, d), F32),
        *rs_set, V((8, rows, d), BF),
        V((nj, m, FCH), F32), V((nj, m, FCH), BF), V((nj, m, FCH), BF),
        V((m, ff), BF), V((m, ff), BF),
        V((4, 2, rows, d), F32), V((4, 2, rows, d), BF), V((4, rows, d), BF), *rs_set,
        D, D((nj,)), D((nj,)), D((NC,)), D((4,)),
        D((nj,)), D((nj,)), D((nj,)), D((nj,)),
        *([D((2, NC))] * 2), *([D((2, NC, 4))] * 2), *([D((NC, 4))] * 4),
    ]
    hbm = pl.BlockSpec(memory_space=pl.ANY)
    vm = pl.BlockSpec(memory_space=pltpu.VMEM)
    flops = 2 * m * d * ff * 6
    return pl.pallas_call(
        kernel,
        out_shape=(
            jax.ShapeDtypeStruct((rows, d), BF), jax.ShapeDtypeStruct((rows, d), BF),
            jax.ShapeDtypeStruct((m, ff), BF), jax.ShapeDtypeStruct((8, rows, d), BF),
            jax.ShapeDtypeStruct((m, ff), BF), jax.ShapeDtypeStruct((m, ff), BF),
        ),
        in_specs=[hbm, vm, hbm, hbm, hbm],
        out_specs=(vm, vm, hbm, hbm, hbm, hbm),
        scratch_shapes=scratch,
        compiler_params=pltpu.CompilerParams(
            collective_id=0, has_side_effects=True, vmem_limit_bytes=62 * 1024 * 1024
        ),
        cost_estimate=pl.CostEstimate(flops=flops, bytes_accessed=6 * d * ff, transcendentals=m * ff),
        name="chain",
    )(tokens, teacher, gate_weight, up_weight, down_weight)


def grads_kernel(tok, hid, ds, dg, du, gg, gu, gd):
    t = tok[...]
    gg[...] = tn(t, dg[...]).astype(BF)
    gu[...] = tn(t, du[...]).astype(BF)
    gd[...] = tn(hid[...], ds[...]).astype(BF)


def weight_grads(tokens, hid, ds, dg, du):
    m, d = tokens.shape
    ff = hid.shape[1]
    steps = 8
    return pl.pallas_call(
        grads_kernel,
        grid=(steps,),
        out_shape=(
            jax.ShapeDtypeStruct((d, ff), BF), jax.ShapeDtypeStruct((d, ff), BF),
            jax.ShapeDtypeStruct((ff, d), BF),
        ),
        in_specs=[
            pl.BlockSpec((m, d // steps), lambda i: (0, i)),
            pl.BlockSpec((m, ff // steps), lambda i: (0, i)),
            pl.BlockSpec((m, d), lambda i: (0, 0)),
            pl.BlockSpec((m, ff), lambda i: (0, 0)),
            pl.BlockSpec((m, ff), lambda i: (0, 0)),
        ],
        out_specs=(
            pl.BlockSpec((d // steps, ff), lambda i: (i, 0)),
            pl.BlockSpec((d // steps, ff), lambda i: (i, 0)),
            pl.BlockSpec((ff // steps, d), lambda i: (i, 0)),
        ),
        compiler_params=pltpu.CompilerParams(vmem_limit_bytes=60 * 1024 * 1024),
        cost_estimate=pl.CostEstimate(flops=6 * m * d * ff, bytes_accessed=6 * d * ff, transcendentals=0),
        name="weight_grads",
    )(tokens, hid, ds, dg, du)


def local_fused(tokens, teacher, gate_weight, up_weight, down_weight):
    out, dtok, hid, ds, dg, du = fused(tokens, teacher, gate_weight, up_weight, down_weight)
    ds = ds.reshape(tokens.shape)
    grad_gate, grad_up, grad_down = weight_grads(tokens, hid, ds, dg, du)
    return out, dtok, grad_gate, grad_up, grad_down


def local(tokens, teacher, gate_weight, up_weight, down_weight):
    local_rows = teacher.shape[0]
    part_gate = jnp.dot(tokens, gate_weight, preferred_element_type=F32)
    part_up = jnp.dot(tokens, up_weight, preferred_element_type=F32)
    gate_proj, up_proj = lax.psum((part_gate, part_up), "col")
    sigmoid_gate = jax.nn.sigmoid(gate_proj)
    activated = gate_proj * sigmoid_gate
    hidden = (activated * up_proj).astype(BF)
    partial_out = jnp.dot(hidden, down_weight, preferred_element_type=F32)
    student = lax.psum(partial_out, "row")
    own_start = lax.axis_index("row") * local_rows
    own_rows = lax.dynamic_slice_in_dim(student, own_start, local_rows, 0)
    student_out = own_rows.astype(BF)
    teacher_all = lax.all_gather(teacher, "row", axis=0, tiled=True)
    d_student = (student - teacher_all.astype(F32)).astype(BF)
    d_hidden = lax.psum(nt(d_student, down_weight), "col")
    grad_down = tn(hidden, d_student).astype(BF)
    d_gate = (d_hidden * up_proj * sigmoid_gate * (1.0 + gate_proj * (1.0 - sigmoid_gate))).astype(BF)
    d_up = (d_hidden * activated).astype(BF)
    grad_gate = tn(tokens, d_gate).astype(BF)
    grad_up = tn(tokens, d_up).astype(BF)
    total = nt(d_gate, gate_weight) + nt(d_up, up_weight)
    d_tokens = lax.psum_scatter(total, "row", scatter_dimension=0, tiled=True).astype(BF)
    return (student_out, d_tokens, grad_gate, grad_up, grad_down)


def solution(mesh):
    placed = (
        P("groups", "col"),
        P(("groups", "row"), "col"),
        P("col", "row"),
        P("col", "row"),
        P("row", "col"),
    )
    small = mesh.shape["row"] == 8 and mesh.shape["col"] == 2
    return jax.shard_map(
        local_fused if small else local,
        mesh=mesh,
        in_specs=placed,
        out_specs=(
            P(("groups", "row"), "col"),
            P(("groups", "row"), "col"),
            P(("groups", "col"), "row"),
            P(("groups", "col"), "row"),
            P(("groups", "row"), "col"),
        ),
        check_vma=False,
    )
```

```python
import jax
import jax.numpy as jnp
from jax import lax
from jax.experimental import pallas as pl
from jax.experimental.pallas import tpu as pltpu
from jax.sharding import PartitionSpec as P

F32 = jnp.float32
BF = jnp.bfloat16
MESH = pl.DeviceIdType.MESH
FCH = 1024
NC = 4
LAG_B = 1
LAG_C = 2


def nt(a, b):
    return lax.dot_general(a, b, (((1,), (1,)), ((), ())), preferred_element_type=F32)


def tn(a, b):
    return lax.dot_general(a, b, (((0,), (0,)), ((), ())), preferred_element_type=F32)


def kernel(
    tokens_h, teacher_ref, wg_h, wu_h, wd_h,
    out_ref, dtok_ref, hid_h, ds_h, dg_h, du_h,
    tok, wg, wu, wd, gp, up, gus, gur, hid,
    pf, pb, xr, sf, zs, zr, dsf, dh, dhs, dhr, dg, du,
    pf2, pb2, xr2, zs2, zr2,
    ld_tok, ld_g, ld_u, ld_d, st,
    gu_ss, gu_rs, dh_ss, dh_rs,
    x_ss, x_rs, z_ss, z_rs, agz_ss, agz_rs, agx_ss, agx_rs,
):
    r = lax.axis_index("row")
    core = lax.axis_index("col")
    z = r // 2
    x = r % 2
    xid = {"row": z * 2 + 1 - x}
    cid = {"col": 1 - core}
    others = [(z + i) % 4 for i in (1, 2, 3)]
    nff = wg.shape[1]
    nd = wd.shape[1]
    nj = nff // FCH
    cw = nd // NC
    dcw = wg.shape[0] // NC

    def fcols(j):
        return pl.ds(pl.multiple_of(j * FCH, FCH), FCH)

    def cols(c):
        return pl.ds(c * cw, cw)

    pltpu.make_async_copy(tokens_h, tok, ld_tok).start()
    for j in range(nj):
        s = pl.ds(j * FCH, FCH)
        pltpu.make_async_copy(wg_h.at[:, s], wg.at[:, s], ld_g.at[j]).start()
        pltpu.make_async_copy(wu_h.at[:, s], wu.at[:, s], ld_u.at[j]).start()
    for c in range(NC):
        pltpu.make_async_copy(wd_h.at[:, cols(c)], wd.at[:, cols(c)], ld_d.at[c]).start()

    barrier = pltpu.get_barrier_semaphore()
    pl.semaphore_signal(barrier, inc=1, device_id=cid, device_id_type=MESH)
    pl.semaphore_signal(barrier, inc=1, device_id=xid, device_id_type=MESH)
    for t in others:
        pl.semaphore_signal(barrier, inc=1, device_id={"row": t * 2 + x}, device_id_type=MESH)
    pl.semaphore_wait(barrier, 5)

    def rc(src, dst, ss, rs, dev):
        return pltpu.make_async_remote_copy(
            src_ref=src, dst_ref=dst, send_sem=ss, recv_sem=rs, device_id=dev, device_id_type=MESH
        )

    def gu_copy(j):
        return rc(gus.at[j], gur.at[j], gu_ss.at[j], gu_rs.at[j], cid)

    pltpu.make_async_copy(tokens_h, tok, ld_tok).wait()

    def first(j, carry):
        s = fcols(j)
        pltpu.make_async_copy(wg_h.at[:, s], wg.at[:, s], ld_g.at[j]).wait()
        pg = jnp.dot(tok[...], wg[:, s], preferred_element_type=F32)
        gp[:, s] = pg
        gus[j, 0] = pg.astype(BF)
        pltpu.make_async_copy(wu_h.at[:, s], wu.at[:, s], ld_u.at[j]).wait()
        pu = jnp.dot(tok[...], wu[:, s], preferred_element_type=F32)
        up[:, s] = pu
        gus[j, 1] = pu.astype(BF)
        gu_copy(j).start()
        return carry

    lax.fori_loop(0, nj, first, 0)

    def second(j, carry):
        s = fcols(j)
        gu_copy(j).wait_recv()
        g = gp[:, s] + gur[j, 0].astype(F32)
        u = up[:, s] + gur[j, 1].astype(F32)
        gp[:, s] = g
        up[:, s] = u
        hid[:, s] = (g * jax.nn.sigmoid(g) * u).astype(BF)
        return carry

    lax.fori_loop(0, nj, second, 0)
    pltpu.make_async_copy(hid, hid_h, st.at[0]).start()

    def x_copy(k, c):
        b, t = (pb, xr) if k == 0 else (pb2, xr2)
        return rc(b.at[:, 1 - x, :, cols(c)], t.at[:, :, cols(c)], x_ss.at[k, c], x_rs.at[k, c], xid)

    def z_send(k, c, t):
        b, s = (zs, zr) if k == 0 else (zs2, zr2)
        return rc(b.at[t, :, cols(c)], s.at[z, :, cols(c)], z_ss.at[k, c, t], z_rs.at[k, c, z], {"row": t * 2 + x})

    def z_recv(k, c, t):
        b, s = (zs, zr) if k == 0 else (zs2, zr2)
        return rc(b.at[t, :, cols(c)], s.at[t, :, cols(c)], z_ss.at[k, c, t], z_rs.at[k, c, t], {"row": t * 2 + x})

    def stage_a(k, c):
        f, t, b = (pf, xr, zs) if k == 0 else (pf2, xr2, zs2)
        q = cols(c)
        x_copy(k, c).wait_recv()
        v = f[:, x, :, q] + t[:, :, q].astype(F32)
        sf[:, :, q] = v
        b[:, :, q] = v.astype(BF)
        for o in others:
            z_send(k, c, o).start()

    def stage_b(k, c, final):
        s = zr if k == 0 else zr2
        q = cols(c)
        v = sf[z, :, q]
        for o in others:
            z_recv(k, c, o).wait_recv()
            v = v + s[o, :, q].astype(F32)
        final(c, v)

    def rs_drain(k):
        for c in range(NC):
            x_copy(k, c).wait_send()
            for o in others:
                z_send(k, c, o).wait_send()

    for c in range(NC):
        q = cols(c)
        pltpu.make_async_copy(wd_h.at[:, q], wd.at[:, q], ld_d.at[c]).wait()
        pc = jnp.dot(hid[...], wd[:, q], preferred_element_type=F32).reshape(4, 2, 32, cw)
        pf[:, :, :, q] = pc
        pb[:, :, :, q] = pc.astype(BF)
        x_copy(0, c).start()

    def factors(j, carry):
        s = fcols(j)
        g = gp[:, s]
        u = up[:, s]
        sg = jax.nn.sigmoid(g)
        gp[:, s] = u * sg * (1.0 + g * (1.0 - sg))
        up[:, s] = g * sg
        return carry

    lax.fori_loop(0, nj, factors, 0)

    def agz_send(c, t):
        b = dsf.at[r, :, cols(c)]
        return rc(b, b, agz_ss.at[c, t], agz_rs.at[c, z], {"row": t * 2 + x})

    def agz_recv(c, t):
        b = dsf.at[t * 2 + x, :, cols(c)]
        return rc(b, b, agz_ss.at[c, t], agz_rs.at[c, t], {"row": t * 2 + x})

    def agx(c, t, src_x):
        b = dsf.at[t * 2 + src_x, :, cols(c)]
        return rc(b, b, agx_ss.at[c, t], agx_rs.at[c, t], xid)

    def student_final(c, v):
        q = cols(c)
        out_ref[:, q] = v.astype(BF)
        dsf[r, :, q] = (v - teacher_ref[:, q].astype(F32)).astype(BF)
        agx(c, z, x).start()
        for o in others:
            agz_send(c, o).start()

    def stage_c(c):
        for o in others:
            agz_recv(c, o).wait_recv()
            agx(c, o, x).start()

    for i in range(NC + LAG_C):
        if i < NC:
            stage_a(0, i)
        if 0 <= i - LAG_B < NC:
            stage_b(0, i - LAG_B, student_final)
        if 0 <= i - LAG_C < NC:
            stage_c(i - LAG_C)
    for c in range(NC):
        for t in range(4):
            agx(c, t, 1 - x).wait_recv()
    ds_copy = pltpu.make_async_copy(dsf, ds_h, st.at[1])
    ds_copy.start()

    def dh_copy(j):
        return rc(dhs.at[j], dhr.at[j], dh_ss.at[j], dh_rs.at[j], cid)

    def third(j, carry):
        p = nt(dsf[...].reshape(256, nd), wd[fcols(j), :])
        dh[j] = p
        dhs[j] = p.astype(BF)
        dh_copy(j).start()
        return carry

    lax.fori_loop(0, nj, third, 0)

    def fourth(j, carry):
        s = fcols(j)
        dh_copy(j).wait_recv()
        d = dh[j] + dhr[j].astype(F32)
        dg[:, s] = (d * gp[:, s]).astype(BF)
        du[:, s] = (d * up[:, s]).astype(BF)
        return carry

    lax.fori_loop(0, nj, fourth, 0)
    pltpu.make_async_copy(dg, dg_h, st.at[2]).start()
    pltpu.make_async_copy(du, du_h, st.at[3]).start()

    for c in range(NC):
        q = cols(c)
        pc = (nt(dg[...], wg[q, :]) + nt(du[...], wu[q, :])).reshape(4, 2, 32, cw)
        pf2[:, :, :, q] = pc
        pb2[:, :, :, q] = pc.astype(BF)
        x_copy(1, c).start()

    def dtok_final(c, v):
        dtok_ref[:, cols(c)] = v.astype(BF)

    for i in range(NC + LAG_B):
        if i < NC:
            stage_a(1, i)
        if i >= LAG_B:
            stage_b(1, i - LAG_B, dtok_final)

    def drain(j, carry):
        gu_copy(j).wait_send()
        dh_copy(j).wait_send()
        return carry

    lax.fori_loop(0, nj, drain, 0)
    rs_drain(0)
    rs_drain(1)
    for c in range(NC):
        for o in others:
            agz_send(c, o).wait_send()
        for t in range(4):
            agx(c, t, x).wait_send()

    for i, (a, b) in enumerate(((hid, hid_h), (dsf, ds_h), (dg, dg_h), (du, du_h))):
        pltpu.make_async_copy(a, b, st.at[i]).wait()


def fused(tokens, teacher, gate_weight, up_weight, down_weight):
    m, d = tokens.shape
    ff = gate_weight.shape[1]
    rows = teacher.shape[0]
    nj = ff // FCH
    V = pltpu.VMEM
    D = pltpu.SemaphoreType.DMA
    rs_set = [V((4, rows, d), BF)] * 2
    scratch = [
        V((m, d), BF), V((d, ff), BF), V((d, ff), BF), V((ff, d), BF),
        V((m, ff), F32), V((m, ff), F32),
        V((nj, 2, m, FCH), BF), V((nj, 2, m, FCH), BF), V((m, ff), BF),
        V((4, 2, rows, d), F32), V((4, 2, rows, d), BF), V((4, rows, d), BF), V((4, rows, d), F32),
        *rs_set, V((8, rows, d), BF),
        V((nj, m, FCH), F32), V((nj, m, FCH), BF), V((nj, m, FCH), BF),
        V((m, ff), BF), V((m, ff), BF),
        V((4, 2, rows, d), F32), V((4, 2, rows, d), BF), V((4, rows, d), BF), *rs_set,
        D, D((nj,)), D((nj,)), D((NC,)), D((4,)),
        D((nj,)), D((nj,)), D((nj,)), D((nj,)),
        *([D((2, NC))] * 2), *([D((2, NC, 4))] * 2), *([D((NC, 4))] * 4),
    ]
    hbm = pl.BlockSpec(memory_space=pl.ANY)
    vm = pl.BlockSpec(memory_space=pltpu.VMEM)
    flops = 2 * m * d * ff * 6
    return pl.pallas_call(
        kernel,
        out_shape=(
            jax.ShapeDtypeStruct((rows, d), BF), jax.ShapeDtypeStruct((rows, d), BF),
            jax.ShapeDtypeStruct((m, ff), BF), jax.ShapeDtypeStruct((8, rows, d), BF),
            jax.ShapeDtypeStruct((m, ff), BF), jax.ShapeDtypeStruct((m, ff), BF),
        ),
        in_specs=[hbm, vm, hbm, hbm, hbm],
        out_specs=(vm, vm, hbm, hbm, hbm, hbm),
        scratch_shapes=scratch,
        compiler_params=pltpu.CompilerParams(
            collective_id=0, has_side_effects=True, vmem_limit_bytes=62 * 1024 * 1024
        ),
        cost_estimate=pl.CostEstimate(flops=flops, bytes_accessed=6 * d * ff, transcendentals=m * ff),
        name="chain",
    )(tokens, teacher, gate_weight, up_weight, down_weight)


def grads_kernel(tok, hid, ds, dg, du, gg, gu, gd):
    t = tok[...]
    gg[...] = tn(t, dg[...]).astype(BF)
    gu[...] = tn(t, du[...]).astype(BF)
    gd[...] = tn(hid[...], ds[...]).astype(BF)


def weight_grads(tokens, hid, ds, dg, du):
    m, d = tokens.shape
    ff = hid.shape[1]
    steps = 4
    return pl.pallas_call(
        grads_kernel,
        grid=(steps,),
        out_shape=(
            jax.ShapeDtypeStruct((d, ff), BF), jax.ShapeDtypeStruct((d, ff), BF),
            jax.ShapeDtypeStruct((ff, d), BF),
        ),
        in_specs=[
            pl.BlockSpec((m, d // steps), lambda i: (0, i)),
            pl.BlockSpec((m, ff // steps), lambda i: (0, i)),
            pl.BlockSpec((m, d), lambda i: (0, 0)),
            pl.BlockSpec((m, ff), lambda i: (0, 0)),
            pl.BlockSpec((m, ff), lambda i: (0, 0)),
        ],
        out_specs=(
            pl.BlockSpec((d // steps, ff), lambda i: (i, 0)),
            pl.BlockSpec((d // steps, ff), lambda i: (i, 0)),
            pl.BlockSpec((ff // steps, d), lambda i: (i, 0)),
        ),
        compiler_params=pltpu.CompilerParams(vmem_limit_bytes=60 * 1024 * 1024),
        cost_estimate=pl.CostEstimate(flops=6 * m * d * ff, bytes_accessed=6 * d * ff, transcendentals=0),
        name="weight_grads",
    )(tokens, hid, ds, dg, du)


def local_fused(tokens, teacher, gate_weight, up_weight, down_weight):
    out, dtok, hid, ds, dg, du = fused(tokens, teacher, gate_weight, up_weight, down_weight)
    ds = ds.reshape(tokens.shape)
    grad_gate, grad_up, grad_down = weight_grads(tokens, hid, ds, dg, du)
    return out, dtok, grad_gate, grad_up, grad_down


def local(tokens, teacher, gate_weight, up_weight, down_weight):
    local_rows = teacher.shape[0]
    part_gate = jnp.dot(tokens, gate_weight, preferred_element_type=F32)
    part_up = jnp.dot(tokens, up_weight, preferred_element_type=F32)
    gate_proj, up_proj = lax.psum((part_gate, part_up), "col")
    sigmoid_gate = jax.nn.sigmoid(gate_proj)
    activated = gate_proj * sigmoid_gate
    hidden = (activated * up_proj).astype(BF)
    partial_out = jnp.dot(hidden, down_weight, preferred_element_type=F32)
    student = lax.psum(partial_out, "row")
    own_start = lax.axis_index("row") * local_rows
    own_rows = lax.dynamic_slice_in_dim(student, own_start, local_rows, 0)
    student_out = own_rows.astype(BF)
    teacher_all = lax.all_gather(teacher, "row", axis=0, tiled=True)
    d_student = (student - teacher_all.astype(F32)).astype(BF)
    d_hidden = lax.psum(nt(d_student, down_weight), "col")
    grad_down = tn(hidden, d_student).astype(BF)
    d_gate = (d_hidden * up_proj * sigmoid_gate * (1.0 + gate_proj * (1.0 - sigmoid_gate))).astype(BF)
    d_up = (d_hidden * activated).astype(BF)
    grad_gate = tn(tokens, d_gate).astype(BF)
    grad_up = tn(tokens, d_up).astype(BF)
    total = nt(d_gate, gate_weight) + nt(d_up, up_weight)
    d_tokens = lax.psum_scatter(total, "row", scatter_dimension=0, tiled=True).astype(BF)
    return (student_out, d_tokens, grad_gate, grad_up, grad_down)


def solution(mesh):
    placed = (
        P("groups", "col"),
        P(("groups", "row"), "col"),
        P("col", "row"),
        P("col", "row"),
        P("row", "col"),
    )
    small = mesh.shape["row"] == 8 and mesh.shape["col"] == 2
    return jax.shard_map(
        local_fused if small else local,
        mesh=mesh,
        in_specs=placed,
        out_specs=(
            P(("groups", "row"), "col"),
            P(("groups", "row"), "col"),
            P(("groups", "col"), "row"),
            P(("groups", "col"), "row"),
            P(("groups", "row"), "col"),
        ),
        check_vma=False,
    )
```
